32 devices in a mesh: gx: 4 (over y, core), gy: 8 (over z, x).
Axes of the slice: x: 2, y: 2, z: 4, core: 2. Of those that a mesh axis runs over, the one named last changes fastest.
Arguments:
- raw_window: float32 [2048, 16384], P('gx', 'gy'), may hold values from -6 to 6
- source_ids: int32 [256], P(('gx', 'gy')), may hold values from 0 to 2047, as said below
- pair_source: int32 [4096], P(('gx', 'gy')), may hold values from 0 to 255
- pair_holder: int32 [4096, 1], P(('gx', 'gy')), may hold values from 0 to 31; in each aligned block of 128 rows (0 to 127, 128 to 255, ...) at most 8 rows name the same one
- pair_receiver: int32 [4096], P(('gx', 'gy')), may hold values from 0 to 63
Outputs:
- correlations: float32 [4096, 512], P(('gx', 'gy'))
The draws below stay inside these ranges and needn't reach their ends.
Inputs may be any that keep to these rules, and one draw needn't show every extreme that they name: The ids are distinct, and source k is a channel of the device that holds channels from (k // 8) * 64 on: source_ids[k] // 64 == k // 8. `pair_holder`: among the 128 pairs of one device, at most 8 name the same holder, a bound that some block reaches; every device is named by some pair.
All inputs are finite; a program needn't handle non-finite values.
Results may differ from the reference program's by a relative error of at most 0.0095.
Values may be sent and summed in bfloat16 or wider, within the bound.
A program may use at most 128 MiB of HBM per device.

```python
import math
import jax
import jax.numpy as jnp
import numpy as np
from jax import lax

NBIN = 2048
SEGLEN = 4096
NSEG = 4
BAND = 64
NLAG = 512
VS = 256
CH_DEV = 64
PAIRS_DEV = 128
CHANNELS = 2048
TIME = 16384
SRC_DEV = 8
CAP = 8
PAIRS = 4096
N_GX = 4
N_GY = 8


def draw_source_ids(key, part):
    blocks = VS // SRC_DEV
    scores = jax.random.randint(key, (blocks, CH_DEV), 0, 1 << 20)
    scores = scores * CH_DEV + jnp.arange(CH_DEV, dtype=jnp.int32)[None, :]
    order = jnp.argsort(scores, axis=1, stable=True)[:, :SRC_DEV].astype(jnp.int32)
    offsets = CH_DEV * jnp.arange(blocks, dtype=jnp.int32)[:, None]
    return (order + offsets).reshape(VS).astype(jnp.int32)


def plant(result, rng, low, high):
    index_at = [jax.random.randint(jax.random.fold_in(rng, axis), (), 0, length) for axis, length in enumerate(result.shape)]
    main_axis = result.shape.index(max(result.shape))
    neighbour = index_at[:main_axis] + [(index_at[main_axis] + 1) % result.shape[main_axis]] + index_at[main_axis + 1:]
    return result.at[tuple(index_at)].set(low).at[tuple(neighbour)].set(high)


def block_scale(stream_key, dims, pieces, smallest, high):
    loudness = 1.0
    for position, blocks in pieces:
        heights = jax.random.uniform(jax.random.fold_in(jax.random.fold_in(stream_key, 6), position), (blocks,), jnp.float32, smallest / len(pieces), high / len(pieces))
        loudness = loudness * jnp.repeat(jnp.exp(heights), dims[position] // blocks).reshape((-1,) + (1,) * (len(dims) - 1 - position))
    return loudness


def rank_bounds(count, slope):
    loads = [(1 << 20) // math.isqrt(rank ** slope) + 1 for rank in range(1, count + 1)]
    scale = 1 + sum(loads) // (1 << 30)
    return np.cumsum(np.array([max(1, weight // scale) for weight in loads]))


def skewed_ids(rng, extent, amount, skew):
    grid = rank_bounds(amount, skew)
    lot = jax.random.randint(jax.random.fold_in(rng, 1), extent, 0, int(grid[amount - 1]))
    rank = jnp.searchsorted(jnp.asarray(grid, jnp.int32), lot, side="right")
    return jax.random.permutation(jax.random.fold_in(rng, 2), amount)[rank].astype(jnp.int32)


def deal_out(key, own, number, rows, number_of, top, bound, lean):
    ranking = jax.random.permutation(key, number_of)
    crowded, ordinary = load_shares(number_of, rows * top, bound, lean, True), load_shares(number_of, rows * top, bound, lean, False)
    places = jnp.arange(number_of)

    def named(lengths, turn):
        used = int((lengths > 0).sum())
        fixed = max(1, used // 4)
        passed = fixed + (places - fixed + turn * (used - fixed)) % max(1, number_of - fixed)
        return jnp.zeros((number_of,), jnp.int32).at[ranking[jnp.where(places < fixed, places, passed)]].set(jnp.asarray(lengths, jnp.int32))

    lengths = jnp.where(number % 4 == 0, named(crowded, number // 4), named(ordinary, number - number // 4 - 1))
    mixed = jax.random.permutation(jax.random.fold_in(own, 3), number_of)
    source_of, receiver = mixed[0:number_of // 2 * 2:2], mixed[1:number_of // 2 * 2:2]
    room = jnp.minimum(lengths[source_of] - 1, bound - lengths[receiver]) // 2
    room = jnp.where((source_of == ranking[0]) | (receiver == ranking[0]) | (lengths[receiver] == 0), 0, jnp.maximum(room, 0))
    passed = jax.random.randint(jax.random.fold_in(own, 4), (number_of // 2,), 0, 1 << 20) % (room + 1)
    lengths = lengths.at[source_of].add(-passed).at[receiver].add(passed)
    items = jnp.searchsorted(jnp.cumsum(lengths), jnp.arange(rows * top), side="right").astype(jnp.int32)
    table = items.reshape(top, rows).T
    table = table[jax.random.permutation(jax.random.fold_in(own, 1), rows)]
    turn = jax.random.randint(jax.random.fold_in(own, 2), (rows, 1), 0, top)
    return jnp.take_along_axis(table, (jnp.arange(top)[None, :] + turn) % top, axis=1)


def load_shares(count, total, most, skew, full):
    weights = [(1 << 20) // math.isqrt(grade ** skew) + 1 for grade in range(1, count + 1)]
    largest = most if full else min(most, max(-(-total // count), total * weights[0] // sum(weights)))
    least = 1 if total - largest >= count - 1 else 0
    counts, surplus = [largest] + [least] * (count - 1), total - largest - least * (count - 1)
    while surplus > 0:
        free = [i for i in range(1, count) if counts[i] < largest] or [i for i in range(1, count) if counts[i] < most]
        pool, budget = sum([weights[i] for i in free]), surplus
        for i in free:
            addition = min(most - counts[i], max(1, budget * weights[i] // pool), surplus)
            counts[i] = counts[i] + addition
            surplus = surplus - addition
    return np.array(counts)


def normal_values(stream_key, dims, deviation, most, shards=(), kind=jnp.bfloat16):
    values = deviation * jax.random.normal(stream_key, dims, jnp.float32)
    if shards:
        values = values * block_scale(stream_key, dims, shards, -0.22, 0.18)
    return jnp.clip(values, -most, most).astype(kind)


def setup_inputs(seed: int = 0) -> dict:
    streams_of = jax.random.split(jax.random.key(seed), 6)
    raw_window = normal_values(streams_of[0], (CHANNELS, TIME), 1.0, 6.0, ((0, 4), (1, 8)), jnp.float32)
    source_ids = draw_source_ids(jax.random.fold_in(streams_of[5], 71), 0)
    pair_source = plant(skewed_ids(streams_of[2], (PAIRS,), VS, 2), jax.random.fold_in(streams_of[2], 3), 0, VS - 1).astype(jnp.int32)
    pair_holder_keys = jax.random.split(jax.random.fold_in(streams_of[3], 1), PAIRS // PAIRS_DEV)
    pair_holder_turns = jax.random.permutation(jax.random.fold_in(streams_of[3], 3), PAIRS // PAIRS_DEV)
    pair_holder = jax.vmap(lambda own, number: deal_out(jax.random.fold_in(streams_of[3], 2), own, number, PAIRS_DEV, N_GX * N_GY, 1, CAP, 2))(pair_holder_keys, pair_holder_turns).reshape((PAIRS, 1))
    pair_receiver = plant(jax.random.randint(streams_of[4], (PAIRS,), 0, CH_DEV), jax.random.fold_in(streams_of[4], 1), 0, CH_DEV - 1).astype(jnp.int32)
    return {"raw_window": raw_window, "source_ids": source_ids, "pair_source": pair_source, "pair_holder": pair_holder, "pair_receiver": pair_receiver}


def inverse_table():
    bins = jnp.arange(NBIN, dtype=jnp.int32)
    lags = (jnp.arange(NLAG, dtype=jnp.int32) - NLAG // 2) % SEGLEN
    phase = bins[:, None] * lags[None, :] % SEGLEN
    angle = phase.astype(jnp.float32) * (2.0 * math.pi / SEGLEN)
    weight = jnp.where(bins == 0, 1.0, 2.0).astype(jnp.float32) * (0.5 / math.sqrt(NSEG * NBIN))
    return jnp.concatenate([weight[:, None] * jnp.cos(angle), -weight[:, None] * jnp.sin(angle)], axis=0)

def reference(raw_window, source_ids, pair_source, pair_holder, pair_receiver):
    samples = jnp.arange(SEGLEN, dtype=jnp.float32)
    taper = jnp.sin(math.pi * (samples + 0.5) / SEGLEN) ** 2

    def whiten(block):
        tapered = (block.reshape(CH_DEV, NSEG, SEGLEN) * taper).astype(jnp.bfloat16)
        spectrum = jnp.fft.rfft(tapered.astype(jnp.float32), axis=-1)[..., :NBIN]
        real_part = jnp.real(spectrum)
        imag_part = jnp.imag(spectrum)
        power = (real_part * real_part + imag_part * imag_part).reshape(CH_DEV, NSEG, NBIN // BAND, BAND)
        level = jnp.sqrt(lax.optimization_barrier(jnp.mean(power, axis=3)) + 1e-06)
        level = jnp.repeat(level, BAND, axis=2)
        return jnp.stack([real_part / level, imag_part / level], axis=2).astype(jnp.bfloat16)
    whitened = lax.map(whiten, raw_window.reshape(CHANNELS // CH_DEV, CH_DEV, TIME))
    whitened = whitened.reshape(CHANNELS, NSEG, 2, NBIN)
    receiver_channel = (pair_holder[:, 0] * CH_DEV + pair_receiver).astype(jnp.int32)
    source_channel = jnp.take(source_ids, pair_source).astype(jnp.int32)
    table = inverse_table()

    def pair_block(indices):
        source_rows = jnp.take(whitened, indices[0], axis=0).astype(jnp.float32)
        receiver_rows = jnp.take(whitened, indices[1], axis=0).astype(jnp.float32)
        real_part = lax.optimization_barrier(jnp.sum(source_rows[:, :, 0] * receiver_rows[:, :, 0] + source_rows[:, :, 1] * receiver_rows[:, :, 1], axis=1))
        imag_part = lax.optimization_barrier(jnp.sum(source_rows[:, :, 1] * receiver_rows[:, :, 0] - source_rows[:, :, 0] * receiver_rows[:, :, 1], axis=1))
        cross = jnp.concatenate([real_part, imag_part], axis=1).astype(jnp.bfloat16)
        return jnp.dot(cross.astype(jnp.float32), table, precision=lax.Precision.HIGHEST, preferred_element_type=jnp.float32)
    blocks = PAIRS // PAIRS_DEV
    indices = jnp.stack([source_channel.reshape(blocks, PAIRS_DEV), receiver_channel.reshape(blocks, PAIRS_DEV)], axis=1)
    return lax.map(pair_block, indices).reshape(PAIRS, NLAG)
```

```python
import functools
import math

import jax
import jax.numpy as jnp
import ml_dtypes
import numpy as np
from jax import lax
from jax.experimental import pallas as pl
from jax.experimental.pallas import tpu as pltpu
from jax.sharding import Mesh, PartitionSpec as P

NBIN = 2048
SEGLEN = 4096
NSEG = 4
BAND = 64
NLAG = 512
HALF = SEGLEN // 2
STEPS = 4
BANDS = NBIN // BAND // STEPS
WIDE = NBIN // 2 // STEPS
COLS = 4 * WIDE
BF16 = ml_dtypes.bfloat16
EVERY = ("gx", "seg", "part")


def step_bins(step):
    col = np.arange(WIDE)
    even = BAND * (step * BANDS + col % BANDS) + 2 * (col // BANDS)
    return even, even + 1


@functools.lru_cache(None)
def forward_tables():
    times = np.arange(HALF)
    tables = []
    for parity in range(2):
        steps = []
        for step in range(STEPS):
            angle = (times[:, None] * step_bins(step)[parity][None, :] % SEGLEN) * (2.0 * math.pi / SEGLEN)
            steps.append(np.concatenate([np.cos(angle), -np.sin(angle)], axis=1))
        tables.append(np.stack(steps).astype(BF16))
    return tables


@functools.lru_cache(None)
def inverse_table():
    lags = (np.arange(NLAG) - NLAG // 2) % SEGLEN
    rows = []
    for step in range(STEPS):
        for bins in step_bins(step):
            angle = (bins[:, None] * lags[None, :] % SEGLEN) * (2.0 * math.pi / SEGLEN)
            weight = np.where(bins == 0, 1.0, 2.0)[:, None] * (0.5 / math.sqrt(NSEG * NBIN))
            rows += [weight * np.cos(angle), -weight * np.sin(angle)]
    return np.concatenate(rows, axis=0).astype(BF16)


def dot(a, b):
    return jnp.dot(a, b, preferred_element_type=jnp.float32)


def whiten_kernel(first_ref, second_ref, sign_ref, pick_ref, even_ref, odd_ref, white_ref, mine_ref, sums, diffs):
    @pl.when(pl.program_id(0) == 0)
    def _():
        first = first_ref[...].astype(jnp.float32)
        second = second_ref[...].astype(jnp.float32)
        sums[...] = (first + second).astype(jnp.bfloat16)
        diffs[...] = ((first - second) * sign_ref[0, 0]).astype(jnp.bfloat16)

    even = dot(sums[...], even_ref[0])
    odd = dot(diffs[...], odd_ref[0])
    power = even * even + odd * odd
    total = power[:, 0:128]
    for lane in range(128, 2 * WIDE, 128):
        total = total + power[:, lane:lane + 128]
    shift = 64
    while shift >= BANDS:
        total = total + pltpu.roll(total, shift, 1)
        shift //= 2
    scale = lax.rsqrt(total * (1.0 / BAND) + 1e-06)
    scale = jnp.concatenate([scale] * (2 * WIDE // 128), axis=1)
    white = jnp.concatenate([even * scale, odd * scale], axis=1).astype(jnp.bfloat16)
    white_ref[...] = white
    rows = white.shape[0]
    chosen = pick_ref[...] == lax.broadcasted_iota(jnp.int32, (pick_ref.shape[0], rows), 1)
    mine_ref[...] = dot(chosen.astype(jnp.bfloat16), white).astype(jnp.bfloat16)


def whiten(first, second, sign, pick):
    even, odd = forward_tables()
    rows, count = first.shape[0], pick.shape[0]
    whole = lambda shape: pl.BlockSpec(shape, lambda g: (0, 0))
    return pl.pallas_call(
        whiten_kernel,
        grid=(STEPS,),
        in_specs=[
            whole((rows, HALF)),
            whole((rows, HALF)),
            pl.BlockSpec(memory_space=pltpu.SMEM),
            whole((count, 1)),
            pl.BlockSpec((1, HALF, 2 * WIDE), lambda g: (g, 0, 0)),
            pl.BlockSpec((1, HALF, 2 * WIDE), lambda g: (g, 0, 0)),
        ],
        out_specs=[
            pl.BlockSpec((rows, COLS), lambda g: (0, g)),
            pl.BlockSpec((count, COLS), lambda g: (0, g)),
        ],
        out_shape=[
            jax.ShapeDtypeStruct((rows, STEPS * COLS), jnp.bfloat16),
            jax.ShapeDtypeStruct((count, STEPS * COLS), jnp.bfloat16),
        ],
        scratch_shapes=[pltpu.VMEM((rows, HALF), jnp.bfloat16), pltpu.VMEM((rows, HALF), jnp.bfloat16)],
        compiler_params=pltpu.CompilerParams(vmem_limit_bytes=40 * 1024 * 1024),
        name="whiten",
    )(first, second, sign, pick, jnp.asarray(even), jnp.asarray(odd))


def correlate_kernel(source_ref, receiver_ref, sources_ref, white_ref, table_ref, out_ref):
    tile = source_ref.shape[0]
    ids = lax.broadcasted_iota(jnp.int32, (tile, sources_ref.shape[0]), 1)
    rows = lax.broadcasted_iota(jnp.int32, (tile, white_ref.shape[0]), 1)
    source = (source_ref[...] == ids).astype(jnp.bfloat16)
    receiver = (receiver_ref[...] == rows).astype(jnp.bfloat16)
    total = jnp.zeros((tile, NLAG), jnp.float32)
    for step in range(2 * STEPS):
        columns = slice(step * 2 * WIDE, (step + 1) * 2 * WIDE)
        a = dot(source, sources_ref[:, columns])
        b = dot(receiver, white_ref[:, columns])
        ar, ai, br, bi = a[:, :WIDE], a[:, WIDE:], b[:, :WIDE], b[:, WIDE:]
        cross = jnp.concatenate([ar * br + ai * bi, ai * br - ar * bi], axis=1).astype(jnp.bfloat16)
        total = total + dot(cross, table_ref[columns, :])
    out_ref[...] = total.astype(jnp.bfloat16)


def correlate(source, receiver, sources, white):
    slots = source.shape[0]
    tile = math.gcd(slots, 256)
    whole = lambda shape: pl.BlockSpec(shape, lambda g: (0, 0))
    return pl.pallas_call(
        correlate_kernel,
        grid=(slots // tile,),
        in_specs=[
            pl.BlockSpec((tile, 1), lambda g: (g, 0)),
            pl.BlockSpec((tile, 1), lambda g: (g, 0)),
            whole(sources.shape),
            whole(white.shape),
            whole((2 * NBIN, NLAG)),
        ],
        out_specs=pl.BlockSpec((tile, NLAG), lambda g: (g, 0)),
        out_shape=jax.ShapeDtypeStruct((slots, NLAG), jnp.bfloat16),
        compiler_params=pltpu.CompilerParams(vmem_limit_bytes=40 * 1024 * 1024),
        name="correlate",
    )(source, receiver, sources, white, jnp.asarray(inverse_table()))


def body(raw_window, source_ids, pair_source, pair_holder, pair_receiver):
    gx, seg, part = (lax.axis_index(name) for name in EVERY)
    parts = lax.axis_size("part")
    groups = NSEG * parts
    devices = lax.axis_size("gx") * groups
    channels, span = raw_window.shape
    rows = channels // parts
    block = channels // groups
    pairs = pair_source.shape[0]
    slots = 2 * pairs // devices

    holder = pair_holder[:, 0]
    order = jnp.arange(pairs, dtype=jnp.int32)
    same = (holder[:, None] == holder[None, :]) & (order[None, :] < order[:, None])
    slot = holder * slots + jnp.sum(same.astype(jnp.int32), axis=1)
    wanted = jnp.stack([pair_source, holder % NSEG * block + pair_receiver], axis=0)
    spots = jnp.arange(devices * slots, dtype=jnp.int32)
    match = slot[None, :] == spots[:, None]
    outgoing = jnp.max(jnp.where(match[None], wanted[:, None, :], -1), axis=2)
    packed = jnp.concatenate([outgoing.reshape(-1), source_ids])
    asked = lax.all_gather(packed, EVERY, axis=0)
    near = NSEG * slots
    start = (gx * parts + part) * near
    requests = asked[:, :2 * devices * slots].reshape(devices, 2, devices * slots)
    requests = lax.dynamic_slice_in_dim(requests, start, near, axis=2)
    asked_source = requests[:, 0].reshape(devices * near, 1)
    asked_receiver = requests[:, 1].reshape(devices * near, 1)
    picks = asked[:, 2 * devices * slots:]
    picks = lax.dynamic_slice_in_dim(picks, (gx * parts + part) * NSEG, NSEG, axis=0)
    pick = picks.reshape(-1, 1) - gx * channels - part * rows

    samples = part * span + jnp.arange(span, dtype=jnp.int32)
    taper = jnp.sin(math.pi * (samples.astype(jnp.float32) + 0.5) / SEGLEN) ** 2
    tapered = (raw_window * taper[None, :]).astype(jnp.bfloat16)
    if parts == 2:
        first = lax.dynamic_slice_in_dim(tapered, part * rows, rows, axis=0)
        away = lax.dynamic_slice_in_dim(tapered, (1 - part) * rows, rows, axis=0)
        second = lax.ppermute(away, "part", [(0, 1), (1, 0)])
        sign = jnp.where(part == 0, 1.0, -1.0).astype(jnp.float32).reshape(1, 1)
    else:
        segment = lax.all_to_all(tapered, "part", split_axis=0, concat_axis=1, tiled=True)
        first, second = segment[:, :HALF], segment[:, HALF:]
        sign = jnp.ones((1, 1), jnp.float32)
    white, mine = whiten(first, second, sign, pick)
    sources = lax.all_gather(mine, ("gx", "part"), axis=0, tiled=True)
    partial = correlate(asked_source, asked_receiver, sources, white)
    returned = lax.all_to_all(partial, EVERY, split_axis=0, concat_axis=0, tiled=True)

    keys = spots.reshape(devices // groups, 1, parts, near)
    keys = jnp.broadcast_to(keys, (devices // groups, NSEG, parts, near)).reshape(-1)
    chosen = (slot[:, None] == keys[None, :]).astype(jnp.bfloat16)
    return dot(chosen, returned)


def solution(mesh):
    n_gx, n_gy = mesh.devices.shape
    fine = Mesh(mesh.devices.reshape(n_gx, NSEG, n_gy // NSEG), EVERY)
    whole = P(EVERY)
    return jax.shard_map(
        body,
        mesh=fine,
        in_specs=(P("gx", ("seg", "part")), whole, whole, P(EVERY, None), whole),
        out_specs=P(EVERY, None),
        check_vma=False,
    )
```

```python
import functools
import math

import jax
import jax.numpy as jnp
import ml_dtypes
import numpy as np
from jax import lax
from jax.experimental import pallas as pl
from jax.experimental.pallas import tpu as pltpu
from jax.sharding import Mesh, PartitionSpec as P

NBIN = 2048
SEGLEN = 4096
NSEG = 4
BAND = 64
NLAG = 512
HALF = SEGLEN // 2
STEPS = 4
BANDS = NBIN // BAND // STEPS
WIDE = NBIN // 2 // STEPS
COLS = 4 * WIDE
BF16 = ml_dtypes.bfloat16
MESH = pl.DeviceIdType.MESH
EVERY = ("gx", "seg", "part")


def step_bins(step):
    col = np.arange(WIDE)
    even = BAND * (step * BANDS + col % BANDS) + 2 * (col // BANDS)
    return even, even + 1


@functools.lru_cache(None)
def forward_tables():
    times = np.arange(HALF)
    tables = []
    for parity in range(2):
        steps = []
        for step in range(STEPS):
            angle = (times[:, None] * step_bins(step)[parity][None, :] % SEGLEN) * (2.0 * math.pi / SEGLEN)
            steps.append(np.concatenate([np.cos(angle), -np.sin(angle)], axis=1))
        tables.append(np.stack(steps).astype(BF16))
    return tables


@functools.lru_cache(None)
def inverse_table():
    lags = (np.arange(NLAG) - NLAG // 2) % SEGLEN
    rows = []
    for step in range(STEPS):
        for bins in step_bins(step):
            angle = (bins[:, None] * lags[None, :] % SEGLEN) * (2.0 * math.pi / SEGLEN)
            weight = np.where(bins == 0, 1.0, 2.0)[:, None] * (0.5 / math.sqrt(NSEG * NBIN))
            rows += [weight * np.cos(angle), -weight * np.sin(angle)]
    return np.concatenate(rows, axis=0).astype(BF16)


def dot(a, b):
    return jnp.dot(a, b, preferred_element_type=jnp.float32)


def whiten_kernel(first_ref, second_ref, sign_ref, pick_ref, even_ref, odd_ref, white_ref, mine_ref, sums, diffs):
    @pl.when(pl.program_id(0) == 0)
    def _():
        first = first_ref[...].astype(jnp.float32)
        second = second_ref[...].astype(jnp.float32)
        sums[...] = (first + second).astype(jnp.bfloat16)
        diffs[...] = ((first - second) * sign_ref[0, 0]).astype(jnp.bfloat16)

    even = dot(sums[...], even_ref[0])
    odd = dot(diffs[...], odd_ref[0])
    power = even * even + odd * odd
    total = power[:, 0:128]
    for lane in range(128, 2 * WIDE, 128):
        total = total + power[:, lane:lane + 128]
    shift = 64
    while shift >= BANDS:
        total = total + pltpu.roll(total, shift, 1)
        shift //= 2
    scale = lax.rsqrt(total * (1.0 / BAND) + 1e-06)
    scale = jnp.concatenate([scale] * (2 * WIDE // 128), axis=1)
    white = jnp.concatenate([even * scale, odd * scale], axis=1).astype(jnp.bfloat16)
    white_ref[...] = white
    rows = white.shape[0]
    chosen = pick_ref[...] == lax.broadcasted_iota(jnp.int32, (pick_ref.shape[0], rows), 1)
    mine_ref[...] = dot(chosen.astype(jnp.bfloat16), white).astype(jnp.bfloat16)


def whiten(first, second, sign, pick):
    even, odd = forward_tables()
    rows, count = first.shape[0], pick.shape[0]
    whole = lambda shape: pl.BlockSpec(shape, lambda g: (0, 0))
    return pl.pallas_call(
        whiten_kernel,
        grid=(STEPS,),
        in_specs=[
            whole((rows, HALF)),
            whole((rows, HALF)),
            pl.BlockSpec(memory_space=pltpu.SMEM),
            whole((count, 1)),
            pl.BlockSpec((1, HALF, 2 * WIDE), lambda g: (g, 0, 0)),
            pl.BlockSpec((1, HALF, 2 * WIDE), lambda g: (g, 0, 0)),
        ],
        out_specs=[
            pl.BlockSpec((rows, COLS), lambda g: (0, g)),
            pl.BlockSpec((count, COLS), lambda g: (0, g)),
        ],
        out_shape=[
            jax.ShapeDtypeStruct((rows, STEPS * COLS), jnp.bfloat16),
            jax.ShapeDtypeStruct((count, STEPS * COLS), jnp.bfloat16),
        ],
        scratch_shapes=[pltpu.VMEM((rows, HALF), jnp.bfloat16), pltpu.VMEM((rows, HALF), jnp.bfloat16)],
        compiler_params=pltpu.CompilerParams(vmem_limit_bytes=40 * 1024 * 1024),
        name="whiten",
    )(first, second, sign, pick, jnp.asarray(even), jnp.asarray(odd))


def spread_kernel(n_gx, parts, mine_ref, out_ref, send, recv, pass_send, pass_recv):
    gx, part = lax.axis_index("gx"), lax.axis_index("part")
    half = n_gx // 2
    row, core = lax.div(gx, 2), lax.rem(gx, 2)
    sibling = {"gx": gx + 1 - 2 * core}
    moves = [(i, j) for i in range(half) for j in range(parts) if i or j]

    def at(i, j):
        return lax.rem(row + i, half) * 2 + core, lax.rem(part + j, parts)

    barrier = pltpu.get_barrier_semaphore()
    for i, j in moves:
        there, where = at(i, j)
        pl.semaphore_signal(barrier, inc=1, device_id={"gx": there, "part": where}, device_id_type=MESH)
    pl.semaphore_signal(barrier, inc=1, device_id=sibling, device_id_type=MESH)
    pl.semaphore_wait(barrier, len(moves) + 1)

    def copy(src, index, sems, device):
        return pltpu.make_async_remote_copy(
            src_ref=src, dst_ref=out_ref.at[index], send_sem=sems[0], recv_sem=sems[1],
            device_id=device, device_id_type=MESH,
        )

    me = gx * parts + part
    started = []
    for n, (i, j) in enumerate(moves):
        there, where = at(i, j)
        started.append(copy(mine_ref, me, (send.at[n], recv.at[n]), {"gx": there, "part": where}))
        started[-1].start()
    last = len(moves)
    started.append(copy(mine_ref, me, (pass_send.at[last], pass_recv.at[last]), sibling))
    started[-1].start()
    out_ref[me] = mine_ref[...]
    other = sibling["gx"] - gx
    arrivals = [copy(mine_ref, me + other * parts, (pass_send.at[last], pass_recv.at[last]), sibling)]
    for n, (i, j) in enumerate(moves):
        there, where = at(half - i, parts - j)
        index = there * parts + where
        copy(mine_ref, index, (send.at[n], recv.at[n]), sibling).wait_recv()
        started.append(copy(out_ref.at[index], index, (pass_send.at[n], pass_recv.at[n]), sibling))
        started[-1].start()
        arrivals.append(copy(mine_ref, index + other * parts, (pass_send.at[n], pass_recv.at[n]), sibling))
    for one in arrivals:
        one.wait_recv()
    for one in started:
        one.wait_send()


def spread(mine):
    n_gx, parts = lax.axis_size("gx"), lax.axis_size("part")
    blocks = n_gx * parts
    count = blocks // 2
    out = pl.pallas_call(
        functools.partial(spread_kernel, n_gx, parts),
        in_specs=[pl.BlockSpec(memory_space=pltpu.VMEM)],
        out_specs=pl.BlockSpec(memory_space=pltpu.VMEM),
        out_shape=jax.ShapeDtypeStruct((blocks,) + mine.shape, mine.dtype),
        scratch_shapes=[pltpu.SemaphoreType.DMA((count,)) for _ in range(4)],
        compiler_params=pltpu.CompilerParams(collective_id=0, has_side_effects=True, vmem_limit_bytes=16 * 1024 * 1024),
        name="spread",
    )(mine)
    return out.reshape(blocks * mine.shape[0], mine.shape[1])


def correlate_kernel(n_gx, parts, source_ref, receiver_ref, sources_ref, white_ref, table_ref, landed_ref, staged, send, recv):
    gx, seg, part = (lax.axis_index(name) for name in EVERY)
    groups = NSEG * parts
    devices, near = landed_ref.shape[0], landed_ref.shape[1]
    me = (gx * NSEG + seg) * parts + part

    def place(device):
        rest = lax.rem(device, groups)
        return {"gx": lax.div(device, groups), "seg": lax.div(rest, parts), "part": lax.rem(rest, parts)}

    barrier = pltpu.get_barrier_semaphore()

    def greet(n, _):
        there = place(lax.rem(me + n, devices))
        pl.semaphore_signal(barrier, inc=1, device_id=there, device_id_type=MESH)
        return _

    lax.fori_loop(1, devices, greet, 0)
    pl.semaphore_wait(barrier, devices - 1)

    def copy(src, dst, device):
        return pltpu.make_async_remote_copy(
            src_ref=staged.at[src], dst_ref=landed_ref.at[dst], send_sem=send.at[src], recv_sem=recv.at[dst],
            device_id=place(device), device_id_type=MESH,
        )

    per = min(devices, max(1, 256 // near))
    tiles = devices // per
    tile = per * near
    ids = lax.broadcasted_iota(jnp.int32, (tile, sources_ref.shape[0]), 1)
    rows = lax.broadcasted_iota(jnp.int32, (tile, white_ref.shape[0]), 1)

    def one_tile(t, _):
        owner = lax.rem(lax.div(me, per) + 1 + t, tiles) * per
        span = pl.ds(pl.multiple_of(owner * near, tile), tile)
        source = (source_ref[span, :] == ids).astype(jnp.bfloat16)
        receiver = (receiver_ref[span, :] == rows).astype(jnp.bfloat16)
        total = jnp.zeros((tile, NLAG), jnp.float32)
        for step in range(2 * STEPS):
            columns = slice(step * 2 * WIDE, (step + 1) * 2 * WIDE)
            a = dot(source, sources_ref[:, columns])
            b = dot(receiver, white_ref[:, columns])
            ar, ai, br, bi = a[:, :WIDE], a[:, WIDE:], b[:, :WIDE], b[:, WIDE:]
            cross = jnp.concatenate([ar * br + ai * bi, ai * br - ar * bi], axis=1).astype(jnp.bfloat16)
            total = total + dot(cross, table_ref[columns, :])
        staged[pl.ds(owner, per)] = total.astype(jnp.bfloat16).reshape(per, near, NLAG)

        def push(n, _):
            target = owner + lax.rem(lax.rem(me, per) + n, per)

            @pl.when(target != me)
            def _():
                copy(target, me, target).start()
            return 0

        return lax.fori_loop(0, per, push, 0)

    lax.fori_loop(0, tiles, one_tile, 0)
    landed_ref[me] = staged[me]

    def finish(n, _):
        there = lax.rem(me + n, devices)
        copy(there, there, there).wait_recv()
        copy(there, there, there).wait_send()
        return 0

    lax.fori_loop(1, devices, finish, 0)


def correlate(source, receiver, sources, white):
    n_gx, parts = lax.axis_size("gx"), lax.axis_size("part")
    devices = n_gx * NSEG * parts
    near = source.shape[0] // devices
    shape = (devices, near, NLAG)
    out = pl.pallas_call(
        functools.partial(correlate_kernel, n_gx, parts),
        in_specs=[pl.BlockSpec(memory_space=pltpu.VMEM)] * 5,
        out_specs=pl.BlockSpec(memory_space=pltpu.VMEM),
        out_shape=jax.ShapeDtypeStruct(shape, jnp.bfloat16),
        scratch_shapes=[
            pltpu.VMEM(shape, jnp.bfloat16),
            pltpu.SemaphoreType.DMA((devices,)),
            pltpu.SemaphoreType.DMA((devices,)),
        ],
        compiler_params=pltpu.CompilerParams(collective_id=1, has_side_effects=True, vmem_limit_bytes=40 * 1024 * 1024),
        name="correlate",
    )(source, receiver, sources, white, jnp.asarray(inverse_table()))
    return out.reshape(devices * near, NLAG)


def body(raw_window, source_ids, pair_source, pair_holder, pair_receiver):
    gx, seg, part = (lax.axis_index(name) for name in EVERY)
    parts = lax.axis_size("part")
    groups = NSEG * parts
    devices = lax.axis_size("gx") * groups
    channels, span = raw_window.shape
    rows = channels // parts
    block = channels // groups
    pairs = pair_source.shape[0]
    slots = 2 * pairs // devices

    holder = pair_holder[:, 0]
    order = jnp.arange(pairs, dtype=jnp.int32)
    same = (holder[:, None] == holder[None, :]) & (order[None, :] < order[:, None])
    slot = holder * slots + jnp.sum(same.astype(jnp.int32), axis=1)
    near = NSEG * slots
    spots = jnp.arange(devices * slots, dtype=jnp.int32).reshape(devices // groups, 1, parts, near)
    keys = jnp.broadcast_to(spots, (devices // groups, NSEG, parts, near)).reshape(devices, near)
    wanted = jnp.stack([pair_source, holder % NSEG * block + pair_receiver], axis=0)
    match = keys[:, None, :, None] == slot
    outgoing = jnp.max(jnp.where(match, wanted[None, :, None, :], -1), axis=3)
    own = jnp.broadcast_to(source_ids[None, :], (devices, source_ids.shape[0]))
    outgoing = jnp.concatenate([outgoing.reshape(devices, 2 * near), own], axis=1)
    asked = lax.all_to_all(outgoing, EVERY, split_axis=0, concat_axis=0, tiled=True)
    asked_source = asked[:, :near].reshape(devices * near, 1)
    asked_receiver = asked[:, near:2 * near].reshape(devices * near, 1)
    picks = lax.dynamic_slice_in_dim(asked[:, 2 * near:], gx * groups + part * NSEG, NSEG, axis=0)
    pick = picks.reshape(-1, 1) - gx * channels - part * rows

    samples = part * span + jnp.arange(span, dtype=jnp.int32)
    taper = jnp.sin(math.pi * (samples.astype(jnp.float32) + 0.5) / SEGLEN) ** 2
    tapered = (raw_window * taper[None, :]).astype(jnp.bfloat16)
    if parts == 2:
        first = lax.dynamic_slice_in_dim(tapered, part * rows, rows, axis=0)
        away = lax.dynamic_slice_in_dim(tapered, (1 - part) * rows, rows, axis=0)
        second = lax.ppermute(away, "part", [(0, 1), (1, 0)])
        sign = jnp.where(part == 0, 1.0, -1.0).astype(jnp.float32).reshape(1, 1)
    else:
        segment = lax.all_to_all(tapered, "part", split_axis=0, concat_axis=1, tiled=True)
        first, second = segment[:, :HALF], segment[:, HALF:]
        sign = jnp.ones((1, 1), jnp.float32)
    white, mine = whiten(first, second, sign, pick)
    sources = spread(mine)
    returned = correlate(asked_source, asked_receiver, sources, white)

    chosen = (slot[:, None] == keys.reshape(1, -1)).astype(jnp.bfloat16)
    return dot(chosen, returned)


def solution(mesh):
    n_gx, n_gy = mesh.devices.shape
    fine = Mesh(mesh.devices.reshape(n_gx, NSEG, n_gy // NSEG), EVERY)
    whole = P(EVERY)
    return jax.shard_map(
        body,
        mesh=fine,
        in_specs=(P("gx", ("seg", "part")), whole, whole, P(EVERY, None), whole),
        out_specs=P(EVERY, None),
        check_vma=False,
    )
```

```python
import functools
import math

import jax
import jax.numpy as jnp
import ml_dtypes
import numpy as np
from jax import lax
from jax.experimental import pallas as pl
from jax.experimental.pallas import tpu as pltpu
from jax.sharding import Mesh, PartitionSpec as P

NBIN = 2048
SEGLEN = 4096
NSEG = 4
BAND = 64
NLAG = 512
HALF = SEGLEN // 2
STEPS = 4
BANDS = NBIN // BAND // STEPS
WIDE = NBIN // 2 // STEPS
COLS = 4 * WIDE
BF16 = ml_dtypes.bfloat16
MESH = pl.DeviceIdType.MESH
EVERY = ("gx", "seg", "part")


def step_bins(step):
    col = np.arange(WIDE)
    even = BAND * (step * BANDS + col % BANDS) + 2 * (col // BANDS)
    return even, even + 1


@functools.lru_cache(None)
def forward_tables():
    times = np.arange(HALF)
    tables = []
    for parity in range(2):
        steps = []
        for step in range(STEPS):
            angle = (times[:, None] * step_bins(step)[parity][None, :] % SEGLEN) * (2.0 * math.pi / SEGLEN)
            steps.append(np.concatenate([np.cos(angle), -np.sin(angle)], axis=1))
        tables.append(np.stack(steps).astype(BF16))
    return tables


@functools.lru_cache(None)
def inverse_table():
    lags = (np.arange(NLAG) - NLAG // 2) % SEGLEN
    rows = []
    for step in range(STEPS):
        for bins in step_bins(step):
            angle = (bins[:, None] * lags[None, :] % SEGLEN) * (2.0 * math.pi / SEGLEN)
            weight = np.where(bins == 0, 1.0, 2.0)[:, None] * (0.5 / math.sqrt(NSEG * NBIN))
            rows += [weight * np.cos(angle), -weight * np.sin(angle)]
    return np.concatenate(rows, axis=0).astype(BF16)


def dot(a, b):
    return jnp.dot(a, b, preferred_element_type=jnp.float32)


def whiten_step(sums, diffs, even_table, odd_table):
    even = dot(sums, even_table)
    odd = dot(diffs, odd_table)
    power = even * even + odd * odd
    total = power[:, 0:128]
    for lane in range(128, 2 * WIDE, 128):
        total = total + power[:, lane:lane + 128]
    shift = 64
    while shift >= BANDS:
        total = total + pltpu.roll(total, shift, 1)
        shift //= 2
    scale = lax.rsqrt(total * (1.0 / BAND) + 1e-06)
    scale = jnp.concatenate([scale] * (2 * WIDE // 128), axis=1)
    return jnp.concatenate([even * scale, odd * scale], axis=1).astype(jnp.bfloat16)


def whiten_kernel(first_ref, second_ref, even_ref, odd_ref, white_ref, sums, diffs):
    @pl.when(pl.program_id(0) == 0)
    def _():
        first = first_ref[...].astype(jnp.float32)
        second = second_ref[...].astype(jnp.float32)
        sums[...] = (first + second).astype(jnp.bfloat16)
        diffs[...] = (first - second).astype(jnp.bfloat16)

    white_ref[...] = whiten_step(sums[...], diffs[...], even_ref[0], odd_ref[0])


def whiten(first, second):
    even, odd = forward_tables()
    rows = first.shape[0]
    whole = pl.BlockSpec((rows, HALF), lambda g: (0, 0))
    table = pl.BlockSpec((1, HALF, 2 * WIDE), lambda g: (g, 0, 0))
    return pl.pallas_call(
        whiten_kernel,
        grid=(STEPS,),
        in_specs=[whole, whole, table, table],
        out_specs=pl.BlockSpec((rows, COLS), lambda g: (0, g)),
        out_shape=jax.ShapeDtypeStruct((rows, STEPS * COLS), jnp.bfloat16),
        scratch_shapes=[pltpu.VMEM((rows, HALF), jnp.bfloat16), pltpu.VMEM((rows, HALF), jnp.bfloat16)],
        compiler_params=pltpu.CompilerParams(vmem_limit_bytes=40 * 1024 * 1024),
        name="whiten",
    )(first, second, jnp.asarray(even), jnp.asarray(odd))


def swap_kernel(raw_ref, taper_ref, even_hbm, odd_hbm, white_ref, leaving, landed, even, odd, load, send, recv):
    part = lax.axis_index("part")
    partner = {"part": 1 - part}
    rows = white_ref.shape[0]
    pieces, piece = leaving.shape[0], leaving.shape[1]
    barrier = pltpu.get_barrier_semaphore()
    pl.semaphore_signal(barrier, inc=1, device_id=partner, device_id_type=MESH)
    loads = [
        pltpu.make_async_copy(even_hbm, even, load.at[0]),
        pltpu.make_async_copy(odd_hbm, odd, load.at[1]),
    ]
    for one in loads:
        one.start()

    def tapered(base, n):
        span = pl.ds(pl.multiple_of(base * rows + n * piece, piece), piece)
        return (raw_ref[span, :] * taper_ref[...]).astype(jnp.bfloat16)

    leaving[0] = tapered(1 - part, 0)
    pl.semaphore_wait(barrier, 1)
    copies = []
    for n in range(pieces):
        if n:
            leaving[n] = tapered(1 - part, n)
        copies.append(pltpu.make_async_remote_copy(
            src_ref=leaving.at[n], dst_ref=landed.at[n], send_sem=send.at[n], recv_sem=recv.at[n],
            device_id=partner, device_id_type=MESH,
        ))
        copies[-1].start()
    sign = (1 - 2 * part).astype(jnp.float32)
    for one in loads:
        one.wait()
    for n in range(pieces):
        first = tapered(part, n).astype(jnp.float32)
        copies[n].wait_recv()
        second = landed[n].astype(jnp.float32)
        sums = (first + second).astype(jnp.bfloat16)
        diffs = ((first - second) * sign).astype(jnp.bfloat16)
        for step in range(STEPS):
            white_ref[n * piece:(n + 1) * piece, step * COLS:(step + 1) * COLS] = whiten_step(
                sums, diffs, even[step], odd[step])
    for one in copies:
        one.wait_send()


def swap(raw_window, taper):
    even, odd = forward_tables()
    channels, span = raw_window.shape
    rows = channels // 2
    pieces = 2
    cost = pl.CostEstimate(flops=4 * rows * HALF * NBIN, bytes_accessed=60 * 1024 * 1024, transcendentals=0)
    return pl.pallas_call(
        swap_kernel,
        in_specs=[pl.BlockSpec(memory_space=pltpu.VMEM)] * 2 + [pl.BlockSpec(memory_space=pl.ANY)] * 2,
        out_specs=pl.BlockSpec(memory_space=pltpu.VMEM),
        out_shape=jax.ShapeDtypeStruct((rows, STEPS * COLS), jnp.bfloat16),
        scratch_shapes=[
            pltpu.VMEM((pieces, rows // pieces, span), jnp.bfloat16),
            pltpu.VMEM((pieces, rows // pieces, span), jnp.bfloat16),
            pltpu.VMEM(even.shape, jnp.bfloat16),
            pltpu.VMEM(odd.shape, jnp.bfloat16),
            pltpu.SemaphoreType.DMA((2,)),
            pltpu.SemaphoreType.DMA((pieces,)),
            pltpu.SemaphoreType.DMA((pieces,)),
        ],
        compiler_params=pltpu.CompilerParams(collective_id=2, has_side_effects=True, vmem_limit_bytes=48 * 1024 * 1024),
        cost_estimate=cost,
        name="swap",
    )(raw_window, taper, jnp.asarray(even), jnp.asarray(odd))


def spread_kernel(n_gx, parts, white_ref, pick_ref, out_ref, mine_ref, send, recv, pass_send, pass_recv):
    gx, part = lax.axis_index("gx"), lax.axis_index("part")
    half = n_gx // 2
    row, core = lax.div(gx, 2), lax.rem(gx, 2)
    sibling = {"gx": gx + 1 - 2 * core}
    moves = [(i, j) for i in range(half) for j in range(parts) if i or j]

    def at(i, j):
        return lax.rem(row + i, half) * 2 + core, lax.rem(part + j, parts)

    barrier = pltpu.get_barrier_semaphore()
    for i, j in moves:
        there, where = at(i, j)
        pl.semaphore_signal(barrier, inc=1, device_id={"gx": there, "part": where}, device_id_type=MESH)
    pl.semaphore_signal(barrier, inc=1, device_id=sibling, device_id_type=MESH)
    chosen = pick_ref[...] == lax.broadcasted_iota(jnp.int32, (pick_ref.shape[0], white_ref.shape[0]), 1)
    chosen = chosen.astype(jnp.bfloat16)
    for step in range(STEPS):
        columns = slice(step * COLS, (step + 1) * COLS)
        mine_ref[:, columns] = dot(chosen, white_ref[:, columns]).astype(jnp.bfloat16)
    pl.semaphore_wait(barrier, len(moves) + 1)

    def copy(src, index, sems, device):
        return pltpu.make_async_remote_copy(
            src_ref=src, dst_ref=out_ref.at[index], send_sem=sems[0], recv_sem=sems[1],
            device_id=device, device_id_type=MESH,
        )

    me = gx * parts + part
    started = []
    for n, (i, j) in enumerate(moves):
        there, where = at(i, j)
        started.append(copy(mine_ref, me, (send.at[n], recv.at[n]), {"gx": there, "part": where}))
        started[-1].start()
    last = len(moves)
    started.append(copy(mine_ref, me, (pass_send.at[last], pass_recv.at[last]), sibling))
    started[-1].start()
    out_ref[me] = mine_ref[...]
    other = sibling["gx"] - gx
    arrivals = [copy(mine_ref, me + other * parts, (pass_send.at[last], pass_recv.at[last]), sibling)]
    for n, (i, j) in enumerate(moves):
        there, where = at(half - i, parts - j)
        index = there * parts + where
        copy(mine_ref, index, (send.at[n], recv.at[n]), sibling).wait_recv()
        started.append(copy(out_ref.at[index], index, (pass_send.at[n], pass_recv.at[n]), sibling))
        started[-1].start()
        arrivals.append(copy(mine_ref, index + other * parts, (pass_send.at[n], pass_recv.at[n]), sibling))
    for one in arrivals:
        one.wait_recv()
    for one in started:
        one.wait_send()


def spread(white, pick):
    shape = (pick.shape[0], white.shape[1])
    n_gx, parts = lax.axis_size("gx"), lax.axis_size("part")
    blocks = n_gx * parts
    count = blocks // 2
    out = pl.pallas_call(
        functools.partial(spread_kernel, n_gx, parts),
        in_specs=[pl.BlockSpec(memory_space=pltpu.VMEM)] * 2,
        out_specs=pl.BlockSpec(memory_space=pltpu.VMEM),
        out_shape=jax.ShapeDtypeStruct((blocks,) + shape, jnp.bfloat16),
        scratch_shapes=[pltpu.VMEM(shape, jnp.bfloat16)] + [pltpu.SemaphoreType.DMA((count,)) for _ in range(4)],
        compiler_params=pltpu.CompilerParams(collective_id=0, has_side_effects=True, vmem_limit_bytes=16 * 1024 * 1024),
        name="spread",
    )(white, pick)
    return out.reshape(blocks * shape[0], shape[1])


def correlate_kernel(n_gx, parts, source_ref, receiver_ref, sources_ref, white_ref, table_ref, landed_ref, staged, send, recv):
    gx, seg, part = (lax.axis_index(name) for name in EVERY)
    groups = NSEG * parts
    devices, near = landed_ref.shape[0], landed_ref.shape[1]
    me = (gx * NSEG + seg) * parts + part

    def place(device):
        rest = lax.rem(device, groups)
        return {"gx": lax.div(device, groups), "seg": lax.div(rest, parts), "part": lax.rem(rest, parts)}

    barrier = pltpu.get_barrier_semaphore()

    def greet(n, _):
        there = place(lax.rem(me + n, devices))
        pl.semaphore_signal(barrier, inc=1, device_id=there, device_id_type=MESH)
        return _

    lax.fori_loop(1, devices, greet, 0)
    pl.semaphore_wait(barrier, devices - 1)

    def copy(src, dst, device):
        return pltpu.make_async_remote_copy(
            src_ref=staged.at[src], dst_ref=landed_ref.at[dst], send_sem=send.at[src], recv_sem=recv.at[dst],
            device_id=place(device), device_id_type=MESH,
        )

    per = min(devices, max(1, 256 // near))
    tiles = devices // per
    tile = per * near
    ids = lax.broadcasted_iota(jnp.int32, (tile, sources_ref.shape[0]), 1)
    rows = lax.broadcasted_iota(jnp.int32, (tile, white_ref.shape[0]), 1)

    def one_tile(t, _):
        owner = lax.rem(lax.div(me, per) + 1 + t, tiles) * per
        span = pl.ds(pl.multiple_of(owner * near, tile), tile)
        source = (source_ref[span, :] == ids).astype(jnp.bfloat16)
        receiver = (receiver_ref[span, :] == rows).astype(jnp.bfloat16)
        total = jnp.zeros((tile, NLAG), jnp.float32)
        for step in range(2 * STEPS):
            columns = slice(step * 2 * WIDE, (step + 1) * 2 * WIDE)
            a = dot(source, sources_ref[:, columns])
            b = dot(receiver, white_ref[:, columns])
            ar, ai, br, bi = a[:, :WIDE], a[:, WIDE:], b[:, :WIDE], b[:, WIDE:]
            cross = jnp.concatenate([ar * br + ai * bi, ai * br - ar * bi], axis=1).astype(jnp.bfloat16)
            total = total + dot(cross, table_ref[columns, :])
        staged[pl.ds(owner, per)] = total.astype(jnp.bfloat16).reshape(per, near, NLAG)

        def push(n, _):
            target = owner + lax.rem(lax.rem(me, per) + n, per)

            @pl.when(target != me)
            def _():
                copy(target, me, target).start()
            return 0

        return lax.fori_loop(0, per, push, 0)

    lax.fori_loop(0, tiles, one_tile, 0)
    landed_ref[me] = staged[me]

    def finish(n, _):
        there = lax.rem(me + n, devices)
        copy(there, there, there).wait_recv()
        copy(there, there, there).wait_send()
        return 0

    lax.fori_loop(1, devices, finish, 0)


def correlate(source, receiver, sources, white):
    n_gx, parts = lax.axis_size("gx"), lax.axis_size("part")
    devices = n_gx * NSEG * parts
    near = source.shape[0] // devices
    shape = (devices, near, NLAG)
    out = pl.pallas_call(
        functools.partial(correlate_kernel, n_gx, parts),
        in_specs=[pl.BlockSpec(memory_space=pltpu.VMEM)] * 5,
        out_specs=pl.BlockSpec(memory_space=pltpu.VMEM),
        out_shape=jax.ShapeDtypeStruct(shape, jnp.bfloat16),
        scratch_shapes=[
            pltpu.VMEM(shape, jnp.bfloat16),
            pltpu.SemaphoreType.DMA((devices,)),
            pltpu.SemaphoreType.DMA((devices,)),
        ],
        compiler_params=pltpu.CompilerParams(collective_id=1, has_side_effects=True, vmem_limit_bytes=40 * 1024 * 1024),
        name="correlate",
    )(source, receiver, sources, white, jnp.asarray(inverse_table()))
    return out.reshape(devices * near, NLAG)


def body(raw_window, source_ids, pair_source, pair_holder, pair_receiver):
    gx, seg, part = (lax.axis_index(name) for name in EVERY)
    parts = lax.axis_size("part")
    groups = NSEG * parts
    devices = lax.axis_size("gx") * groups
    channels, span = raw_window.shape
    rows = channels // parts
    block = channels // groups
    pairs = pair_source.shape[0]
    slots = 2 * pairs // devices

    holder = pair_holder[:, 0]
    order = jnp.arange(pairs, dtype=jnp.int32)
    same = (holder[:, None] == holder[None, :]) & (order[None, :] < order[:, None])
    slot = holder * slots + jnp.sum(same.astype(jnp.int32), axis=1)
    near = NSEG * slots
    spots = jnp.arange(devices * slots, dtype=jnp.int32).reshape(devices // groups, 1, parts, near)
    keys = jnp.broadcast_to(spots, (devices // groups, NSEG, parts, near)).reshape(devices, near)
    wanted = jnp.stack([pair_source, holder % NSEG * block + pair_receiver], axis=0)
    match = keys[:, None, :, None] == slot
    outgoing = jnp.max(jnp.where(match, wanted[None, :, None, :], -1), axis=3)
    own = jnp.broadcast_to(source_ids[None, :], (devices, source_ids.shape[0]))
    outgoing = jnp.concatenate([outgoing.reshape(devices, 2 * near), own], axis=1)
    asked = lax.all_to_all(outgoing, EVERY, split_axis=0, concat_axis=0, tiled=True)
    asked_source = asked[:, :near].reshape(devices * near, 1)
    asked_receiver = asked[:, near:2 * near].reshape(devices * near, 1)
    picks = lax.dynamic_slice_in_dim(asked[:, 2 * near:], gx * groups + part * NSEG, NSEG, axis=0)
    pick = picks.reshape(-1, 1) - gx * channels - part * rows

    samples = part * span + jnp.arange(span, dtype=jnp.int32)
    taper = jnp.sin(math.pi * (samples.astype(jnp.float32) + 0.5) / SEGLEN) ** 2
    if parts == 2:
        white = swap(raw_window, taper[None, :])
    else:
        tapered = (raw_window * taper[None, :]).astype(jnp.bfloat16)
        segment = lax.all_to_all(tapered, "part", split_axis=0, concat_axis=1, tiled=True)
        white = whiten(segment[:, :HALF], segment[:, HALF:])
    sources = spread(white, pick)
    returned = correlate(asked_source, asked_receiver, sources, white)

    chosen = (slot[:, None] == keys.reshape(1, -1)).astype(jnp.bfloat16)
    return dot(chosen, returned)


def solution(mesh):
    n_gx, n_gy = mesh.devices.shape
    fine = Mesh(mesh.devices.reshape(n_gx, NSEG, n_gy // NSEG), EVERY)
    whole = P(EVERY)
    return jax.shard_map(
        body,
        mesh=fine,
        in_specs=(P("gx", ("seg", "part")), whole, whole, P(EVERY, None), whole),
        out_specs=P(EVERY, None),
        check_vma=False,
    )
```

```python
import functools
import math

import jax
import jax.numpy as jnp
import ml_dtypes
import numpy as np
from jax import lax
from jax.experimental import pallas as pl
from jax.experimental.pallas import tpu as pltpu
from jax.sharding import Mesh, PartitionSpec as P

NBIN = 2048
SEGLEN = 4096
NSEG = 4
BAND = 64
NLAG = 512
HALF = SEGLEN // 2
STEPS = 4
BANDS = NBIN // BAND // STEPS
WIDE = NBIN // 2 // STEPS
COLS = 4 * WIDE
BF16 = ml_dtypes.bfloat16
MESH = pl.DeviceIdType.MESH
EVERY = ("gx", "seg", "part")


def step_bins(step):
    col = np.arange(WIDE)
    even = BAND * (step * BANDS + col % BANDS) + 2 * (col // BANDS)
    return even, even + 1


@functools.lru_cache(None)
def forward_tables():
    times = np.arange(HALF)
    tables = []
    for parity in range(2):
        steps = []
        for step in range(STEPS):
            angle = (times[:, None] * step_bins(step)[parity][None, :] % SEGLEN) * (2.0 * math.pi / SEGLEN)
            steps.append(np.concatenate([np.cos(angle), -np.sin(angle)], axis=1))
        tables.append(np.stack(steps).astype(BF16))
    return tables


@functools.lru_cache(None)
def inverse_table():
    lags = (np.arange(NLAG) - NLAG // 2) % SEGLEN
    rows = []
    for step in range(STEPS):
        for bins in step_bins(step):
            angle = (bins[:, None] * lags[None, :] % SEGLEN) * (2.0 * math.pi / SEGLEN)
            weight = np.where(bins == 0, 1.0, 2.0)[:, None] * (0.5 / math.sqrt(NSEG * NBIN))
            rows += [weight * np.cos(angle), -weight * np.sin(angle)]
    return np.concatenate(rows, axis=0).astype(BF16)


def dot(a, b):
    return jnp.dot(a, b, preferred_element_type=jnp.float32)


def place_of(device, parts):
    rest = lax.rem(device, NSEG * parts)
    return {"gx": lax.div(device, NSEG * parts), "seg": lax.div(rest, parts), "part": lax.rem(rest, parts)}


def whiten_step(sums, diffs, even_table, odd_table):
    even = dot(sums, even_table)
    odd = dot(diffs, odd_table)
    power = even * even + odd * odd
    total = power[:, 0:128]
    for lane in range(128, 2 * WIDE, 128):
        total = total + power[:, lane:lane + 128]
    shift = 64
    while shift >= BANDS:
        total = total + pltpu.roll(total, shift, 1)
        shift //= 2
    scale = lax.rsqrt(total * (1.0 / BAND) + 1e-06)
    scale = jnp.concatenate([scale] * (2 * WIDE // 128), axis=1)
    return jnp.concatenate([even * scale, odd * scale], axis=1).astype(jnp.bfloat16)


def whiten_kernel(first_ref, second_ref, even_ref, odd_ref, white_ref, sums, diffs):
    @pl.when(pl.program_id(0) == 0)
    def _():
        first = first_ref[...].astype(jnp.float32)
        second = second_ref[...].astype(jnp.float32)
        sums[...] = (first + second).astype(jnp.bfloat16)
        diffs[...] = (first - second).astype(jnp.bfloat16)

    white_ref[...] = whiten_step(sums[...], diffs[...], even_ref[0], odd_ref[0])


def whiten(first, second):
    even, odd = forward_tables()
    rows = first.shape[0]
    whole = pl.BlockSpec((rows, HALF), lambda g: (0, 0))
    table = pl.BlockSpec((1, HALF, 2 * WIDE), lambda g: (g, 0, 0))
    return pl.pallas_call(
        whiten_kernel,
        grid=(STEPS,),
        in_specs=[whole, whole, table, table],
        out_specs=pl.BlockSpec((rows, COLS), lambda g: (0, g)),
        out_shape=jax.ShapeDtypeStruct((rows, STEPS * COLS), jnp.bfloat16),
        scratch_shapes=[pltpu.VMEM((rows, HALF), jnp.bfloat16), pltpu.VMEM((rows, HALF), jnp.bfloat16)],
        compiler_params=pltpu.CompilerParams(vmem_limit_bytes=40 * 1024 * 1024),
        name="whiten",
    )(first, second, jnp.asarray(even), jnp.asarray(odd))


def swap_kernel(raw_ref, taper_ref, asking_ref, even_hbm, odd_hbm, white_ref, asked_ref, leaving, landed, even, odd,
                load, send, recv, ask_send, ask_recv):
    gx, seg, part = (lax.axis_index(name) for name in EVERY)
    devices, parts = asking_ref.shape[0], 2
    me = (gx * NSEG + seg) * parts + part
    partner = {"part": 1 - part}
    rows = white_ref.shape[0]
    pieces, piece = leaving.shape[0], leaving.shape[1]
    barrier = pltpu.get_barrier_semaphore()

    def greet(n, _):
        there = place_of(lax.rem(me + n, devices), parts)
        pl.semaphore_signal(barrier, inc=1, device_id=there, device_id_type=MESH)
        return _

    lax.fori_loop(1, devices, greet, 0)
    loads = [
        pltpu.make_async_copy(even_hbm, even, load.at[0]),
        pltpu.make_async_copy(odd_hbm, odd, load.at[1]),
    ]
    for one in loads:
        one.start()

    def tapered(base, n):
        span = pl.ds(pl.multiple_of(base * rows + n * piece, piece), piece)
        return (raw_ref[span, :] * taper_ref[...]).astype(jnp.bfloat16)

    leaving[0] = tapered(1 - part, 0)
    pl.semaphore_wait(barrier, devices - 1)
    copies = []
    for n in range(pieces):
        if n:
            leaving[n] = tapered(1 - part, n)
        copies.append(pltpu.make_async_remote_copy(
            src_ref=leaving.at[n], dst_ref=landed.at[n], send_sem=send.at[n], recv_sem=recv.at[n],
            device_id=partner, device_id_type=MESH,
        ))
        copies[-1].start()

    def request(src, dst, device):
        return pltpu.make_async_remote_copy(
            src_ref=asking_ref.at[src], dst_ref=asked_ref.at[dst], send_sem=ask_send.at[src], recv_sem=ask_recv.at[dst],
            device_id=place_of(device, parts), device_id_type=MESH,
        )

    def ask(n, _):
        there = lax.rem(me + n, devices)
        request(there, me, there).start()
        return 0

    lax.fori_loop(1, devices, ask, 0)
    asked_ref[me] = asking_ref[me]
    sign = (1 - 2 * part).astype(jnp.float32)
    for one in loads:
        one.wait()
    for n in range(pieces):
        first = tapered(part, n).astype(jnp.float32)
        copies[n].wait_recv()
        second = landed[n].astype(jnp.float32)
        sums = (first + second).astype(jnp.bfloat16)
        diffs = ((first - second) * sign).astype(jnp.bfloat16)
        for step in range(STEPS):
            white_ref[n * piece:(n + 1) * piece, step * COLS:(step + 1) * COLS] = whiten_step(
                sums, diffs, even[step], odd[step])
    for one in copies:
        one.wait_send()

    def finish(n, _):
        there = lax.rem(me + n, devices)
        request(there, there, there).wait_recv()
        request(there, there, there).wait_send()
        return 0

    lax.fori_loop(1, devices, finish, 0)


def swap(raw_window, taper, outgoing):
    even, odd = forward_tables()
    channels, span = raw_window.shape
    rows = channels // 2
    pieces = 2
    devices = outgoing.shape[0]
    cost = pl.CostEstimate(flops=4 * rows * HALF * NBIN, bytes_accessed=60 * 1024 * 1024, transcendentals=0)
    return pl.pallas_call(
        swap_kernel,
        in_specs=[pl.BlockSpec(memory_space=pltpu.VMEM)] * 3 + [pl.BlockSpec(memory_space=pl.ANY)] * 2,
        out_specs=[pl.BlockSpec(memory_space=pltpu.VMEM)] * 2,
        out_shape=[
            jax.ShapeDtypeStruct((rows, STEPS * COLS), jnp.bfloat16),
            jax.ShapeDtypeStruct(outgoing.shape, jnp.int32),
        ],
        scratch_shapes=[
            pltpu.VMEM((pieces, rows // pieces, span), jnp.bfloat16),
            pltpu.VMEM((pieces, rows // pieces, span), jnp.bfloat16),
            pltpu.VMEM(even.shape, jnp.bfloat16),
            pltpu.VMEM(odd.shape, jnp.bfloat16),
            pltpu.SemaphoreType.DMA((2,)),
            pltpu.SemaphoreType.DMA((pieces,)),
            pltpu.SemaphoreType.DMA((pieces,)),
            pltpu.SemaphoreType.DMA((devices,)),
            pltpu.SemaphoreType.DMA((devices,)),
        ],
        compiler_params=pltpu.CompilerParams(collective_id=2, has_side_effects=True, vmem_limit_bytes=48 * 1024 * 1024),
        cost_estimate=cost,
        name="swap",
    )(raw_window, taper, outgoing, jnp.asarray(even), jnp.asarray(odd))


def spread_kernel(n_gx, parts, white_ref, pick_ref, out_ref, mine_ref, send, recv, pass_send, pass_recv):
    gx, part = lax.axis_index("gx"), lax.axis_index("part")
    half = n_gx // 2
    row, core = lax.div(gx, 2), lax.rem(gx, 2)
    sibling = {"gx": gx + 1 - 2 * core}
    moves = [(i, j) for i in range(half) for j in range(parts) if i or j]

    def at(i, j):
        return lax.rem(row + i, half) * 2 + core, lax.rem(part + j, parts)

    barrier = pltpu.get_barrier_semaphore()
    for i, j in moves:
        there, where = at(i, j)
        pl.semaphore_signal(barrier, inc=1, device_id={"gx": there, "part": where}, device_id_type=MESH)
    pl.semaphore_signal(barrier, inc=1, device_id=sibling, device_id_type=MESH)
    chosen = pick_ref[...] == lax.broadcasted_iota(jnp.int32, (pick_ref.shape[0], white_ref.shape[0]), 1)
    chosen = chosen.astype(jnp.bfloat16)
    for step in range(STEPS):
        columns = slice(step * COLS, (step + 1) * COLS)
        mine_ref[:, columns] = dot(chosen, white_ref[:, columns]).astype(jnp.bfloat16)
    pl.semaphore_wait(barrier, len(moves) + 1)

    def copy(src, index, sems, device):
        return pltpu.make_async_remote_copy(
            src_ref=src, dst_ref=out_ref.at[index], send_sem=sems[0], recv_sem=sems[1],
            device_id=device, device_id_type=MESH,
        )

    me = gx * parts + part
    started = []
    for n, (i, j) in enumerate(moves):
        there, where = at(i, j)
        started.append(copy(mine_ref, me, (send.at[n], recv.at[n]), {"gx": there, "part": where}))
        started[-1].start()
    last = len(moves)
    started.append(copy(mine_ref, me, (pass_send.at[last], pass_recv.at[last]), sibling))
    started[-1].start()
    out_ref[me] = mine_ref[...]
    other = sibling["gx"] - gx
    arrivals = [copy(mine_ref, me + other * parts, (pass_send.at[last], pass_recv.at[last]), sibling)]
    for n, (i, j) in enumerate(moves):
        there, where = at(half - i, parts - j)
        index = there * parts + where
        copy(mine_ref, index, (send.at[n], recv.at[n]), sibling).wait_recv()
        started.append(copy(out_ref.at[index], index, (pass_send.at[n], pass_recv.at[n]), sibling))
        started[-1].start()
        arrivals.append(copy(mine_ref, index + other * parts, (pass_send.at[n], pass_recv.at[n]), sibling))
    for one in arrivals:
        one.wait_recv()
    for one in started:
        one.wait_send()


def spread(white, pick):
    shape = (pick.shape[0], white.shape[1])
    n_gx, parts = lax.axis_size("gx"), lax.axis_size("part")
    blocks = n_gx * parts
    count = blocks // 2
    out = pl.pallas_call(
        functools.partial(spread_kernel, n_gx, parts),
        in_specs=[pl.BlockSpec(memory_space=pltpu.VMEM)] * 2,
        out_specs=pl.BlockSpec(memory_space=pltpu.VMEM),
        out_shape=jax.ShapeDtypeStruct((blocks,) + shape, jnp.bfloat16),
        scratch_shapes=[pltpu.VMEM(shape, jnp.bfloat16)] + [pltpu.SemaphoreType.DMA((count,)) for _ in range(4)],
        compiler_params=pltpu.CompilerParams(collective_id=0, has_side_effects=True, vmem_limit_bytes=16 * 1024 * 1024),
        name="spread",
    )(white, pick)
    return out.reshape(blocks * shape[0], shape[1])


def correlate_kernel(n_gx, parts, source_ref, receiver_ref, sources_ref, white_ref, table_ref, landed_ref, staged, send, recv):
    gx, seg, part = (lax.axis_index(name) for name in EVERY)
    groups = NSEG * parts
    devices, near = landed_ref.shape[0], landed_ref.shape[1]
    me = (gx * NSEG + seg) * parts + part

    def place(device):
        return place_of(device, parts)

    barrier = pltpu.get_barrier_semaphore()

    def greet(n, _):
        there = place(lax.rem(me + n, devices))
        pl.semaphore_signal(barrier, inc=1, device_id=there, device_id_type=MESH)
        return _

    lax.fori_loop(1, devices, greet, 0)
    pl.semaphore_wait(barrier, devices - 1)

    def copy(src, dst, device):
        return pltpu.make_async_remote_copy(
            src_ref=staged.at[src], dst_ref=landed_ref.at[dst], send_sem=send.at[src], recv_sem=recv.at[dst],
            device_id=place(device), device_id_type=MESH,
        )

    per = min(devices, max(1, 256 // near))
    tiles = devices // per
    tile = per * near
    ids = lax.broadcasted_iota(jnp.int32, (tile, sources_ref.shape[0]), 1)
    rows = lax.broadcasted_iota(jnp.int32, (tile, white_ref.shape[0]), 1)

    def one_tile(t, _):
        owner = lax.rem(lax.div(me, per) + 1 + t, tiles) * per
        span = pl.ds(pl.multiple_of(owner * near, tile), tile)
        source = (source_ref[span, :] == ids).astype(jnp.bfloat16)
        receiver = (receiver_ref[span, :] == rows).astype(jnp.bfloat16)
        total = jnp.zeros((tile, NLAG), jnp.float32)
        for step in range(2 * STEPS):
            columns = slice(step * 2 * WIDE, (step + 1) * 2 * WIDE)
            a = dot(source, sources_ref[:, columns])
            b = dot(receiver, white_ref[:, columns])
            ar, ai, br, bi = a[:, :WIDE], a[:, WIDE:], b[:, :WIDE], b[:, WIDE:]
            cross = jnp.concatenate([ar * br + ai * bi, ai * br - ar * bi], axis=1).astype(jnp.bfloat16)
            total = total + dot(cross, table_ref[columns, :])
        staged[pl.ds(owner, per)] = total.astype(jnp.bfloat16).reshape(per, near, NLAG)

        def push(n, _):
            target = owner + lax.rem(lax.rem(me, per) + n, per)

            @pl.when(target != me)
            def _():
                copy(target, me, target).start()
            return 0

        return lax.fori_loop(0, per, push, 0)

    lax.fori_loop(0, tiles, one_tile, 0)
    landed_ref[me] = staged[me]

    def finish(n, _):
        there = lax.rem(me + n, devices)
        copy(there, there, there).wait_recv()
        copy(there, there, there).wait_send()
        return 0

    lax.fori_loop(1, devices, finish, 0)


def correlate(source, receiver, sources, white):
    n_gx, parts = lax.axis_size("gx"), lax.axis_size("part")
    devices = n_gx * NSEG * parts
    near = source.shape[0] // devices
    shape = (devices, near, NLAG)
    out = pl.pallas_call(
        functools.partial(correlate_kernel, n_gx, parts),
        in_specs=[pl.BlockSpec(memory_space=pltpu.VMEM)] * 5,
        out_specs=pl.BlockSpec(memory_space=pltpu.VMEM),
        out_shape=jax.ShapeDtypeStruct(shape, jnp.bfloat16),
        scratch_shapes=[
            pltpu.VMEM(shape, jnp.bfloat16),
            pltpu.SemaphoreType.DMA((devices,)),
            pltpu.SemaphoreType.DMA((devices,)),
        ],
        compiler_params=pltpu.CompilerParams(collective_id=1, has_side_effects=True, vmem_limit_bytes=40 * 1024 * 1024),
        name="correlate",
    )(source, receiver, sources, white, jnp.asarray(inverse_table()))
    return out.reshape(devices * near, NLAG)


def body(raw_window, source_ids, pair_source, pair_holder, pair_receiver):
    gx, seg, part = (lax.axis_index(name) for name in EVERY)
    parts = lax.axis_size("part")
    groups = NSEG * parts
    devices = lax.axis_size("gx") * groups
    channels, span = raw_window.shape
    rows = channels // parts
    block = channels // groups
    pairs = pair_source.shape[0]
    slots = 2 * pairs // devices

    holder = pair_holder[:, 0]
    order = jnp.arange(pairs, dtype=jnp.int32)
    same = (holder[:, None] == holder[None, :]) & (order[None, :] < order[:, None])
    slot = holder * slots + jnp.sum(same.astype(jnp.int32), axis=1)
    near = NSEG * slots
    spots = jnp.arange(devices * slots, dtype=jnp.int32).reshape(devices // groups, 1, parts, near)
    keys = jnp.broadcast_to(spots, (devices // groups, NSEG, parts, near)).reshape(devices, near)
    wanted = jnp.stack([pair_source, holder % NSEG * block + pair_receiver], axis=0)
    match = keys[:, None, :, None] == slot
    outgoing = jnp.max(jnp.where(match, wanted[None, :, None, :], -1), axis=3)
    own = jnp.broadcast_to(source_ids[None, :], (devices, source_ids.shape[0]))
    outgoing = jnp.concatenate([outgoing.reshape(devices, 2 * near), own], axis=1)
    samples = part * span + jnp.arange(span, dtype=jnp.int32)
    taper = jnp.sin(math.pi * (samples.astype(jnp.float32) + 0.5) / SEGLEN) ** 2
    if parts == 2:
        spare = -outgoing.shape[1] % 128
        outgoing = jnp.pad(outgoing, ((0, 0), (0, spare))).reshape(devices, 1, -1)
        white, asked = swap(raw_window, taper[None, :], outgoing)
        asked = asked.reshape(devices, -1)
    else:
        tapered = (raw_window * taper[None, :]).astype(jnp.bfloat16)
        segment = lax.all_to_all(tapered, "part", split_axis=0, concat_axis=1, tiled=True)
        white = whiten(segment[:, :HALF], segment[:, HALF:])
        asked = lax.all_to_all(outgoing, EVERY, split_axis=0, concat_axis=0, tiled=True)
    asked_source = asked[:, :near].reshape(devices * near, 1)
    asked_receiver = asked[:, near:2 * near].reshape(devices * near, 1)
    picks = lax.dynamic_slice_in_dim(asked[:, 2 * near:2 * near + source_ids.shape[0]], gx * groups + part * NSEG, NSEG, axis=0)
    pick = picks.reshape(-1, 1) - gx * channels - part * rows
    sources = spread(white, pick)
    returned = correlate(asked_source, asked_receiver, sources, white)

    chosen = (slot[:, None] == keys.reshape(1, -1)).astype(jnp.bfloat16)
    return dot(chosen, returned)


def solution(mesh):
    n_gx, n_gy = mesh.devices.shape
    fine = Mesh(mesh.devices.reshape(n_gx, NSEG, n_gy // NSEG), EVERY)
    whole = P(EVERY)
    return jax.shard_map(
        body,
        mesh=fine,
        in_specs=(P("gx", ("seg", "part")), whole, whole, P(EVERY, None), whole),
        out_specs=P(EVERY, None),
        check_vma=False,
    )
```
